256 devices in a mesh: blk: 16 (over x_lo, y, core), uly: 16 (over x_hi, z).
Axes of the slice: x: 4 (x_hi: 2, x_lo: 2; x = x_hi * 2 + x_lo), y: 4, z: 8, core: 2. Of those that a mesh axis runs over, the one named last changes fastest.
Arguments:
- query_states: bfloat16 [16384, 8192], P(('blk', 'uly')), may hold values from -16 to 16
- key_states: bfloat16 [16384, 512], P(('blk', 'uly')), may hold values from -6 to 6
- value_states: bfloat16 [16384, 512], P(('blk', 'uly')), may hold values from -6 to 6
- attn_output: bfloat16 [16384, 8192], P(('blk', 'uly')), may hold values from -6 to 6
- grad_output: bfloat16 [16384, 8192], P(('blk', 'uly')), may hold values from -6 to 6
- token_pos: int32 [16384], P(('blk', 'uly')), may hold values from 0 to 16383, as said below
Outputs:
- grad_query: bfloat16 [16384, 8192], P(('blk', 'uly'))
- grad_key: bfloat16 [16384, 512], P(('blk', 'uly'))
- grad_value: bfloat16 [16384, 512], P(('blk', 'uly'))
The draws below stay inside these ranges and needn't reach their ends.
Inputs may be any that keep to these rules, and one draw needn't show every extreme that they name: `token_pos`: token rows form 32 runs of 512 consecutive rows; run c holds the positions p(c) * 512 to p(c) * 512 + 511 in rising order, where p is a permutation of the runs.
All inputs are finite; a program needn't handle non-finite values.
Results may differ from the reference program's by a relative error of at most 0.005.
Values may be sent and summed in bfloat16 or wider, within the bound.
A program may use at most 128 MiB of HBM per device.

```python
import math
import jax
import jax.numpy as jnp
from jax import lax

QH = 64
KVH = 4
HD = 128
WINBLK = 2
QB = 1024
NRUNS = 32
QRUN = 512
SQ = 16384
N_BLK = 16


def run_order(key):
    return jax.random.permutation(jax.random.fold_in(key, 40), NRUNS)


def uniform_pair(key):
    uniform_one = jax.random.uniform(jax.random.fold_in(key, 41), (SQ, KVH * HD), jnp.float32, 1e-06, 1.0)
    uniform_two = jax.random.uniform(jax.random.fold_in(key, 42), (SQ, KVH * HD), jnp.float32, 0.0, 1.0)
    return (uniform_one, uniform_two)


def draw_key_states(key, part):
    uniform_one, uniform_two = uniform_pair(key)
    normal_draw = jnp.sqrt(-2.0 * jnp.log(uniform_one)) * jnp.cos(2.0 * math.pi * uniform_two)
    return normal_draw.astype(jnp.bfloat16)


def draw_query_states(key, part):
    key = jax.random.fold_in(key, 2)
    left_draw = jax.random.uniform(jax.random.fold_in(key, 5), (SQ, QH * HD), jnp.float32, 1e-06, 1.0)
    right_draw = jax.random.uniform(jax.random.fold_in(key, 6), (SQ, QH * HD), jnp.float32, 0.0, 1.0)
    normal_draw = jnp.sqrt(-2.0 * jnp.log(left_draw)) * jnp.cos(2.0 * math.pi * right_draw)
    return normal_draw.astype(jnp.bfloat16)


def draw_token_pos(key, part):
    order_table = run_order(key)
    row_ids = jnp.arange(SQ, dtype=jnp.int32)
    return (order_table[row_ids // QRUN] * QRUN + row_ids % QRUN).astype(jnp.int32)


def block_scale(rng, dims, pieces, least, largest):
    gain = 1.0
    for position, blocks in pieces:
        steps = jax.random.uniform(jax.random.fold_in(jax.random.fold_in(rng, 6), position), (blocks,), jnp.float32, least / len(pieces), largest / len(pieces))
        gain = gain * jnp.repeat(jnp.exp(steps), dims[position] // blocks).reshape((-1,) + (1,) * (len(dims) - 1 - position))
    return gain


def centred(key, shape, width, limit, pieces=(), kind=jnp.bfloat16):
    values = jax.random.normal(key, shape, jnp.float32) * width
    if len(pieces) > 0:
        values = block_scale(key, shape, pieces, -0.22, 0.18) * values
    return jnp.clip(values, min=-limit, max=limit).astype(kind)


def setup_inputs(seed: int = 0) -> dict:
    keys = jax.random.split(jax.random.key(seed), 7)
    query_states = draw_query_states(jax.random.fold_in(keys[6], 71), 0)
    key_states = draw_key_states(jax.random.fold_in(keys[6], 71), 0)
    value_states = centred(keys[2], (SQ, KVH * HD), 1.0, 6.0, ((0, 256),))
    attn_output = centred(keys[3], (SQ, QH * HD), 1.0, 6.0, ((0, 256),))
    grad_output = centred(keys[4], (SQ, QH * HD), 1.0, 6.0, ((0, 256),))
    token_pos = draw_token_pos(jax.random.fold_in(keys[6], 71), 0)
    return dict(query_states=query_states, key_states=key_states, value_states=value_states, attn_output=attn_output, grad_output=grad_output, token_pos=token_pos)


def head_grads(head_parts, allowed):
    query_head, key_head, value_head, output_head, cotan_head = head_parts
    softmax_scale = HD ** -0.5
    scores = jnp.einsum("igd,jd->gij", query_head.astype(jnp.float32), key_head.astype(jnp.float32)) * softmax_scale
    scores = jnp.where(allowed[None], scores, -jnp.inf)
    row_max = jnp.max(scores, axis=2, keepdims=True)
    log_total = row_max + jnp.log(jnp.sum(jnp.exp(scores - row_max), axis=2, keepdims=True))
    weights = jnp.exp(scores - log_total)
    weights_low = lax.optimization_barrier(weights.astype(jnp.bfloat16))
    row_sums = jnp.sum(cotan_head.astype(jnp.float32) * output_head.astype(jnp.float32), axis=2).T
    grad_v = jnp.einsum("gij,igd->jd", weights_low.astype(jnp.float32), cotan_head.astype(jnp.float32))
    weight_grads = jnp.einsum("igd,jd->gij", cotan_head.astype(jnp.float32), value_head.astype(jnp.float32))
    dscore = lax.optimization_barrier((weights * (weight_grads - row_sums[:, :, None])).astype(jnp.bfloat16))
    grad_q = jnp.einsum("gij,jd->igd", dscore.astype(jnp.float32), key_head.astype(jnp.float32)) * softmax_scale
    grad_k = jnp.einsum("gij,igd->jd", dscore.astype(jnp.float32), query_head.astype(jnp.float32)) * softmax_scale
    return grad_q, grad_k, grad_v


def reference(query_states, key_states, value_states, attn_output, grad_output, token_pos):
    group_size = QH // KVH
    window = WINBLK * QB

    def query_rows(array, first_row):
        piece = lax.dynamic_slice_in_dim(array, first_row, QB, 0)
        return piece.reshape(QB, KVH, group_size, HD).transpose(1, 0, 2, 3)

    def one_block(carry, block_index):
        grad_k, grad_v = carry
        first_row = block_index * QB
        starts = [((block_index - offset) % N_BLK) * QB for offset in range(WINBLK)]
        key_part = jnp.concatenate([lax.dynamic_slice_in_dim(key_states, begin, QB, 0) for begin in starts], 0)
        value_part = jnp.concatenate([lax.dynamic_slice_in_dim(value_states, begin, QB, 0) for begin in starts], 0)
        key_positions = jnp.concatenate([lax.dynamic_slice_in_dim(token_pos, begin, QB, 0) for begin in starts], 0)
        query_positions = lax.dynamic_slice_in_dim(token_pos, first_row, QB, 0)
        allowed = key_positions[None, :] <= query_positions[:, None]
        head_parts = (query_rows(query_states, first_row),
                      key_part.reshape(window, KVH, HD).transpose(1, 0, 2),
                      value_part.reshape(window, KVH, HD).transpose(1, 0, 2),
                      query_rows(attn_output, first_row),
                      query_rows(grad_output, first_row))
        grad_q, part_k, part_v = lax.map(lambda parts: head_grads(parts, allowed), head_parts)
        grad_q = grad_q.transpose(1, 0, 2, 3).reshape(QB, QH * HD).astype(jnp.bfloat16)
        part_k = part_k.transpose(1, 0, 2)
        part_v = part_v.transpose(1, 0, 2)
        for offset, begin in enumerate(starts):
            piece_k = part_k[offset * QB:(offset + 1) * QB]
            piece_v = part_v[offset * QB:(offset + 1) * QB]
            grad_k = lax.dynamic_update_slice_in_dim(grad_k, lax.dynamic_slice_in_dim(grad_k, begin, QB, 0) + piece_k, begin, 0)
            grad_v = lax.dynamic_update_slice_in_dim(grad_v, lax.dynamic_slice_in_dim(grad_v, begin, QB, 0) + piece_v, begin, 0)
        return (grad_k, grad_v), grad_q

    empty_grad = jnp.zeros((SQ, KVH, HD), jnp.float32)
    (grad_k, grad_v), grad_q = lax.scan(one_block, (empty_grad, empty_grad), jnp.arange(N_BLK, dtype=jnp.int32))
    grad_query = grad_q.reshape(SQ, QH * HD)
    grad_key = grad_k.reshape(SQ, KVH * HD).astype(jnp.bfloat16)
    grad_value = grad_v.reshape(SQ, KVH * HD).astype(jnp.bfloat16)
    return (grad_query, grad_key, grad_value)
```

```python
import functools

import jax
import jax.numpy as jnp
from jax import lax
from jax.experimental import pallas as pl
from jax.experimental.pallas import tpu as pltpu
from jax.sharding import PartitionSpec as P

MESH = pl.DeviceIdType.MESH
B16 = jnp.bfloat16
F32 = jnp.float32
QH, KVH, HD = 64, 4, 128
G = QH // KVH
T = 64
NZ = 8
R = G * T
NK = 2048
HALF = NK // 2
PREV, OWN = 0, 1
SCALE = HD ** -0.5
LOG2E = 1.4426950408889634
HIDE = -1e30
C1 = 256
UNROLL_HEADS = False
NT = (((1,), (1,)), ((), ()))
NN = (((1,), (0,)), ((), ()))
ORDER = (4, 3, 5, 2, 6, 1, 7, 0)


def dot(a, b, dims=NN):
    return lax.dot_general(a, b, dims, preferred_element_type=F32)


def when(cond, fn):
    if isinstance(cond, bool):
        if cond:
            fn()
    else:
        pl.when(cond)(fn)


def kernel(nblk, q_hbm, g_hbm, o_hbm, k_ref, v_ref, pos_ref, dq_hbm, dk_ref, dv_ref,
           q_v, g_v, o_v, dq_v, kv, posb, mk, qa, ga, qt, gt, kt, p_sc, sc, dq_sc,
           acc, sp_p, rp_p, s_up, s_dn, r_up, r_dn, s_x, r_x,
           in_sem, out_sem, gx_s, gx_r, gu_s, gu_r, gd_s, gd_r, gb_s, gb_r,
           px_s, px_r, pb_s, pb_r, rb_s, rb_r, ru_s, ru_r, rd_s, rd_r, rx_s, rx_r):
    b = lax.axis_index("blk")
    u = lax.axis_index("uly")
    z = lax.rem(u, NZ)
    xh = u // NZ
    up = (b, xh * NZ + lax.rem(z + 1, NZ))
    dn = (b, xh * NZ + lax.rem(z + NZ - 1, NZ))
    xp = (b, (1 - xh) * NZ + z)
    nx = (lax.rem(b + 1, nblk), u)
    pb = (lax.rem(b + nblk - 1, nblk), u)

    def rcopy(src, dst, ss, rs, dev):
        return pltpu.make_async_remote_copy(src_ref=src, dst_ref=dst, send_sem=ss, recv_sem=rs,
                                            device_id=dev, device_id_type=MESH)

    loads = [pltpu.make_async_copy(a, c, in_sem.at[i])
             for i, (a, c) in enumerate(((q_hbm, q_v), (g_hbm, g_v), (o_hbm, o_v)))]
    for c in loads:
        c.start()
    for h in range(KVH):
        kv[h, OWN, 0, 0, 0] = k_ref[:, h * HD:(h + 1) * HD]
        kv[h, OWN, 1, 0, 0] = v_ref[:, h * HD:(h + 1) * HD]
    base = jnp.min(pos_ref[...], axis=1, keepdims=True) - T * z
    posb[OWN, 0] = jnp.broadcast_to(base, (8, 128))

    barrier = pltpu.get_barrier_semaphore()
    for dev in (up, dn, xp, nx, pb):
        pl.semaphore_signal(barrier, inc=1, device_id=dev, device_id_type=MESH)
    pl.semaphore_wait(barrier, 5)

    def gx(h):
        return rcopy(kv.at[h, OWN, :, 0, 0], kv.at[h, OWN, :, 0, 1], gx_s.at[h], gx_r.at[h], xp)

    def gu(h, s):
        src = (NZ - s) % NZ
        if s < 3:
            return rcopy(kv.at[h, OWN, :, src], kv.at[h, OWN, :, src - 1 if src else NZ - 1],
                         gu_s.at[h, s], gu_r.at[h, s], up)
        return rcopy(kv.at[h, OWN, 0, 5], kv.at[h, OWN, 0, 4], gu_s.at[h, s], gu_r.at[h, s], up)

    def gd(h, s):
        if s < 3:
            return rcopy(kv.at[h, OWN, :, s], kv.at[h, OWN, :, s + 1], gd_s.at[h, s], gd_r.at[h, s], dn)
        return rcopy(kv.at[h, OWN, 1, 3], kv.at[h, OWN, 1, 4], gd_s.at[h, s], gd_r.at[h, s], dn)

    def gb(h, d):
        return rcopy(kv.at[h, OWN, :, d], kv.at[h, PREV, :, d], gb_s.at[h], gb_r.at[h], nx)

    def gather_step(h, s):
        if s == 0:
            gx(h).wait_recv()
            gu(h, 0).start()
            gd(h, 0).start()
            gb(h, 0).start()
        else:
            gu(h, s - 1).wait_recv()
            gd(h, s - 1).wait_recv()
            if s < 4:
                gu(h, s).start()
                gd(h, s).start()
                gb(h, NZ - s).start()
                gb(h, s).start()
            else:
                gb(h, 4).start()

    def gather_prev_done(h):
        rcopy(kv.at[h, OWN], kv.at[h, PREV], gb_s.at[h], gb_r.at[h], nx).wait_recv()

    def pos_x():
        return rcopy(posb.at[OWN, 0], posb.at[OWN, 1], px_s, px_r, xp)

    def pos_b():
        return rcopy(posb.at[OWN], posb.at[PREV], pb_s, pb_r, nx)

    gx(0).start()
    pos_x().start()
    for h in range(1, KVH):
        gx(h).start()
    gather_step(0, 0)
    pos_x().wait_recv()
    pos_b().start()

    lane = lax.broadcasted_iota(jnp.int32, (T, 128), 1)
    row = lax.broadcasted_iota(jnp.int32, (T, 128), 0)
    eye = jnp.where(lane == row, 1.0, 0.0).astype(B16)
    ones = jnp.where(lax.broadcasted_iota(jnp.int32, (256, 128), 1) < 3, 1.0, 0.0).astype(B16)
    for g in range(G):
        qa[g * T:(g + 1) * T, HD:] = eye

    for c in loads:
        c.wait()

    def prep_rows(h):
        for g in range(G):
            sl = pl.ds(h * (G * HD) + g * HD if isinstance(h, int) else pl.multiple_of(h * (G * HD) + g * HD, HD), HD)
            rs = pl.ds(g * T, T)
            qa[rs, :HD] = q_v[:, sl]
            gg = g_v[:, sl]
            ga[rs, :HD] = gg
            d = -jnp.sum(gg.astype(F32) * o_v[:, sl].astype(F32), axis=1, keepdims=True)
            d1 = d.astype(B16)
            e = d - d1.astype(F32)
            d2 = e.astype(B16)
            d3 = e - d2.astype(F32)
            ga[rs, HD:] = jnp.where(lane == 0, d1.astype(F32), jnp.where(lane == 1, d2.astype(F32), jnp.where(lane == 2, d3, 0.0))).astype(B16)
        qt[...] = qa[:, :HD].T
        gt[...] = ga[:, :HD].T

    def make_mask(s):
        for d in range(NZ):
            first = T * lax.rem(z + d, NZ)
            for x in range(2):
                kp = posb[s, x, 0:1, :] + first + row
                qp = posb[OWN, 0, 0:1, :] + T * z + lane
                mk[pl.ds(s * HALF + d * 128 + x * T, T), :] = jnp.where(kp <= qp, 0.0, HIDE).astype(B16)

    def rb(h, d):
        return rcopy(sp_p.at[h, d], rp_p.at[h, d], rb_s.at[h], rb_r.at[h, d], pb)

    def r_u(h, s):
        if s == 0:
            return rcopy(s_up.at[h, 0, 0], r_up.at[h, 0, 0], ru_s.at[h, 0], ru_r.at[h, 0], up)
        return rcopy(s_up.at[h, s], r_up.at[h, s], ru_s.at[h, s], ru_r.at[h, s], up)

    def r_d(h, s):
        if s == 0:
            return rcopy(s_dn.at[h, 0, 1], r_dn.at[h, 0, 1], rd_s.at[h, 0], rd_r.at[h, 0], dn)
        return rcopy(s_dn.at[h, s], r_dn.at[h, s], rd_s.at[h, s], rd_r.at[h, s], dn)

    def rx(h):
        return rcopy(s_x.at[h], r_x.at[h], rx_s.at[h], rx_r.at[h], xp)

    def term(h, d, i):
        return acc[h, d, i] + rp_p[h, d, i].astype(F32)

    def reduce_step(h, s):
        if s == 0:
            rb(h, 4).wait_recv()
            s_up[h, 0, 0] = term(h, 4, 0).astype(B16)
            s_dn[h, 0, 1] = term(h, 4, 1).astype(B16)
            r_u(h, 0).start()
            r_d(h, 0).start()
        elif s < 4:
            du, dd = 4 - s, 4 + s
            rb(h, du).wait_recv()
            rb(h, dd).wait_recv()
            r_u(h, s - 1).wait_recv()
            r_d(h, s - 1).wait_recv()
            for i in range(2):
                tu, td = term(h, du, i), term(h, dd, i)
                if s > 1 or i == 0:
                    tu = tu + r_up[h, s - 1, i].astype(F32)
                if s > 1 or i == 1:
                    td = td + r_dn[h, s - 1, i].astype(F32)
                s_up[h, s, i] = tu.astype(B16)
                s_dn[h, s, i] = td.astype(B16)
            r_u(h, s).start()
            r_d(h, s).start()
        elif s == 4:
            rb(h, 0).wait_recv()
            r_u(h, 3).wait_recv()
            r_d(h, 3).wait_recv()
            for i in range(2):
                t = (term(h, 0, i) + r_up[h, 3, i].astype(F32) + r_dn[h, 3, i].astype(F32)).T
                acc[h, 0, i] = t
                s_x[h, i] = t[T:]
            rx(h).start()
        else:
            rx(h).wait_recv()
            cs = pl.ds(h * HD if isinstance(h, int) else pl.multiple_of(h * HD, HD), HD)
            dk_ref[:, cs] = ((acc[h, 0, 0, 0:T, :] + r_x[h, 0]) * SCALE).astype(B16)
            dv_ref[:, cs] = (acc[h, 0, 1, 0:T, :] + r_x[h, 1]).astype(B16)

    cc = SCALE * LOG2E

    def score_chunk(h, r):
        rs = pl.ds(r * C1, C1)
        qc = qa[rs, :]
        ms, ls = [None] * 8, [None] * 8
        for j in (4, 5, 6, 7, 0, 1, 2, 3):
            s_, e = j // 4, j % 4
            js = pl.ds(j * 256, 256)
            kk = kv[h, s_, 0, 2 * e:2 * e + 2].reshape(256, HD)
            s = dot(jnp.concatenate([kk, mk[js, :]], axis=1), qc, NT)
            m = jnp.max(jnp.max(s.reshape(32, 8, C1), axis=0), axis=0, keepdims=True)
            p = jnp.exp2((s - m) * cc)
            p_sc[js, rs] = p
            ms[j] = m
            ls[j] = jnp.sum(jnp.sum(p.reshape(32, 8, C1), axis=0), axis=0, keepdims=True)
        mm = functools.reduce(jnp.maximum, ms)
        cs = [jnp.exp2((m - mm) * cc) for m in ms]
        inv = 1.0 / functools.reduce(jnp.add, [c * l for c, l in zip(cs, ls)])
        for j in range(8):
            sc[j:j + 1, rs] = cs[j] * inv

    def key_tile(h, t):
        d = ORDER[t]
        w = jnp.concatenate([p_sc[pl.ds(s_ * HALF + d * 128, 128), :] * sc[s_ * 4 + d // 2:s_ * 4 + d // 2 + 1, :] for s_ in range(2)], axis=0)
        vt = jnp.concatenate([jnp.concatenate([kv[h, s_, 1, d].reshape(128, HD) for s_ in range(2)], axis=0), ones], axis=1)
        dp = dot(vt, ga[...], NT)
        ds_ = (w * dp).astype(B16)
        pv = dot(gt[...], w.astype(B16), NT)
        pk = dot(qt[...], ds_, NT)
        dq = dot(kt[d], ds_)
        if t == 0:
            dq_sc[...] = dq
        else:
            dq_sc[...] += dq
        for i, a in enumerate((pk, pv)):
            sp_p[h, d, i] = a[:, :128].astype(B16)
            acc[h, d, i] = a[:, 128:]
        rb(h, d).start()

    def head(h):
        more = h < KVH - 1
        later = h > 0

        def g_next(s):
            when(more, lambda: gather_step(h + 1, s))

        def r_last(s):
            when(later, lambda: reduce_step(h - 1, s))

        gather_prev_done(h)
        prep_rows(h)
        for d in range(NZ):
            kt[d] = jnp.concatenate([kv[h, s_, 0, d].reshape(128, HD) for s_ in range(2)], axis=0).T
        score_chunk(h, 0)
        g_next(0)
        r_last(1)
        score_chunk(h, 1)
        r_last(2)
        score_chunk(h, 2)
        g_next(1)
        score_chunk(h, 3)
        r_last(3)
        key_tile(h, 0)
        g_next(2)
        key_tile(h, 1)
        r_last(4)
        key_tile(h, 2)
        g_next(3)
        key_tile(h, 3)
        key_tile(h, 4)
        reduce_step(h, 0)
        g_next(4)
        key_tile(h, 5)
        r_last(5)
        key_tile(h, 6)
        key_tile(h, 7)
        for g in range(0, G, 2):
            dq = (dq_sc[:, g * T:(g + 2) * T] * SCALE).T.astype(B16)
            for e in range(2):
                c0 = h * (G * HD) + (g + e) * HD
                dq_v[:, pl.ds(c0 if isinstance(h, int) else pl.multiple_of(c0, HD), HD)] = dq[e * T:(e + 1) * T]

    for s in range(1, 5):
        gather_step(0, s)
    make_mask(OWN)
    rcopy(posb.at[OWN], posb.at[PREV], pb_s, pb_r, nx).wait_recv()
    make_mask(PREV)

    if UNROLL_HEADS:
        for h in range(KVH):
            head(h)
    else:
        def loop(h, c):
            head(h)
            return c
        lax.fori_loop(0, KVH, loop, 0)

    out = pltpu.make_async_copy(dq_v, dq_hbm, out_sem)
    out.start()
    for s in range(1, 6):
        reduce_step(KVH - 1, s)

    out.wait()
    pos_x().wait_send()
    pos_b().wait_send()
    for h in range(KVH):
        gx(h).wait_send()
        rcopy(kv.at[h, OWN], kv.at[h, PREV], gb_s.at[h], gb_r.at[h], nx).wait_send()
        rcopy(sp_p.at[h], rp_p.at[h], rb_s.at[h], rb_r.at[h, 0], pb).wait_send()
        rx(h).wait_send()
        for s in range(4):
            gu(h, s).wait_send()
            gd(h, s).wait_send()
            r_u(h, s).wait_send()
            r_d(h, s).wait_send()


def solution(mesh):
    nblk = mesh.shape["blk"]
    vm = pl.BlockSpec(memory_space=pltpu.VMEM)
    hb = pl.BlockSpec(memory_space=pl.ANY)
    dma = pltpu.SemaphoreType.DMA

    def local(q, k, v, o, g, pos):
        dt = q.dtype
        return pl.pallas_call(
            functools.partial(kernel, nblk),
            out_shape=(jax.ShapeDtypeStruct((T, QH * HD), dt), jax.ShapeDtypeStruct((T, KVH * HD), dt), jax.ShapeDtypeStruct((T, KVH * HD), dt)),
            in_specs=[hb, hb, hb, vm, vm, vm],
            out_specs=(hb, vm, vm),
            scratch_shapes=[
                pltpu.VMEM((T, QH * HD), B16), pltpu.VMEM((T, QH * HD), B16), pltpu.VMEM((T, QH * HD), B16), pltpu.VMEM((T, QH * HD), B16),
                pltpu.VMEM((KVH, 2, 2, NZ, 2, T, HD), B16),
                pltpu.VMEM((2, 2, 8, 128), jnp.int32),
                pltpu.VMEM((NK, 128), B16),
                pltpu.VMEM((R, 256), B16), pltpu.VMEM((R, 256), B16),
                pltpu.VMEM((HD, R), B16), pltpu.VMEM((HD, R), B16),
                pltpu.VMEM((NZ, HD, 256), B16),
                pltpu.VMEM((NK, R), F32),
                pltpu.VMEM((8, R), F32),
                pltpu.VMEM((HD, R), F32),
                pltpu.VMEM((KVH, NZ, 2, HD, 128), F32),
                pltpu.VMEM((KVH, NZ, 2, HD, 128), B16), pltpu.VMEM((KVH, NZ, 2, HD, 128), B16),
                pltpu.VMEM((KVH, 4, 2, HD, 128), B16), pltpu.VMEM((KVH, 4, 2, HD, 128), B16),
                pltpu.VMEM((KVH, 4, 2, HD, 128), B16), pltpu.VMEM((KVH, 4, 2, HD, 128), B16),
                pltpu.VMEM((KVH, 2, T, HD), F32), pltpu.VMEM((KVH, 2, T, HD), F32),
                dma((3,)), dma,
                dma((KVH,)), dma((KVH,)),
                dma((KVH, 4)), dma((KVH, 4)), dma((KVH, 4)), dma((KVH, 4)),
                dma((KVH,)), dma((KVH,)),
                dma, dma, dma, dma,
                dma((KVH,)), dma((KVH, NZ)),
                dma((KVH, 4)), dma((KVH, 4)), dma((KVH, 4)), dma((KVH, 4)),
                dma((KVH,)), dma((KVH,)),
            ],
            compiler_params=pltpu.CompilerParams(collective_id=0, has_side_effects=True, vmem_limit_bytes=60 * 2 ** 20),
            cost_estimate=pl.CostEstimate(flops=12 * 10 ** 9, bytes_accessed=6 * 10 ** 6, transcendentals=9 * 10 ** 6),
        )(q, g, o, k, v, pos.reshape(1, T))

    spec = P(("blk", "uly"), None)
    return jax.shard_map(local, mesh=mesh, in_specs=(spec,) * 5 + (P(("blk", "uly")),), out_specs=(spec,) * 3, check_vma=False)
```

```python
import functools

import jax
import jax.numpy as jnp
from jax import lax
from jax.experimental import pallas as pl
from jax.experimental.pallas import tpu as pltpu
from jax.sharding import PartitionSpec as P

MESH = pl.DeviceIdType.MESH
B16 = jnp.bfloat16
F32 = jnp.float32
QH, KVH, HD = 64, 4, 128
G = QH // KVH
T = 64
NZ = 8
R = G * T
NK = 2048
HALF = NK // 2
PREV, OWN = 0, 1
SCALE = HD ** -0.5
LOG2E = 1.4426950408889634
HIDE = -1e30
C1 = 256
NT = (((1,), (1,)), ((), ()))
NN = (((1,), (0,)), ((), ()))
ORDER = (4, 3, 5, 2, 6, 1, 7, 0)


def dot(a, b, dims=NN):
    return lax.dot_general(a, b, dims, preferred_element_type=F32)


def kernel(nblk, q_hbm, g_hbm, o_hbm, k_ref, v_ref, pos_ref, dq_hbm, dk_ref, dv_ref,
           q_v, g_v, o_v, dq_v, kv, posb, mk, qa, ga, ds_sc, p_sc, sc, m_sc, l_sc,
           acc, sp_p, rp_p, s_a1, s_a2, r_a1, r_a2, s_b, r_b,
           in_sem, out_sem, gx_s, gx_r, gu_s, gu_r, gd_s, gd_r, gn_s, gn_r, ga_s, gb_s, gc_s, g_r, gc_r, px_s, px_r, pb_s, pb_r,
           rp_s, rp_r, ra_s, ra_r, rb_s, rb_r):
    b = lax.axis_index("blk")
    u = lax.axis_index("uly")
    z = lax.rem(u, NZ)
    xh = u // NZ
    def at(other, step):
        return (b, (1 - xh if other else xh) * NZ + lax.rem(z + step + NZ, NZ))

    near = [at(x, i) for x in (0, 1) for i in (0, 1, -1, 2, -2)][1:]
    xp = at(1, 0)
    nx = (lax.rem(b + 1, nblk), u)
    pb = (lax.rem(b + nblk - 1, nblk), u)

    def rcopy(src, dst, ss, rs, dev):
        return pltpu.make_async_remote_copy(src_ref=src, dst_ref=dst, send_sem=ss, recv_sem=rs,
                                            device_id=dev, device_id_type=MESH)

    loads = [pltpu.make_async_copy(a, c, in_sem.at[i])
             for i, (a, c) in enumerate(((q_hbm, q_v), (g_hbm, g_v), (o_hbm, o_v)))]
    for c in loads:
        c.start()
    for h in range(KVH):
        kv[h, OWN, 0, 0, 0] = k_ref[:, h * HD:(h + 1) * HD]
        kv[h, OWN, 1, 0, 0] = v_ref[:, h * HD:(h + 1) * HD]
    base = jnp.min(pos_ref[...], axis=1, keepdims=True) - T * z
    posb[OWN, 0] = jnp.broadcast_to(base, (8, 128))

    barrier = pltpu.get_barrier_semaphore()
    for dev in near + [nx, pb]:
        pl.semaphore_signal(barrier, inc=1, device_id=dev, device_id_type=MESH)
    pl.semaphore_wait(barrier, 11)

    def g_a(i):
        own = kv.at[0, OWN, i, 0, 0]
        out = [rcopy(own, kv.at[0, OWN, i, 0, 1], ga_s.at[i, 0], g_r.at[i, 0], xp)]
        for n, step in enumerate((2, -2, 1, -1)):
            for x in range(2):
                d = (NZ - step) % NZ
                out.append(rcopy(own, kv.at[0, OWN, i, d, x], ga_s.at[i, 1 + 2 * n + x], g_r.at[i, d], at(x, step)))
        return out

    def g_b(i):
        lo, hi = kv.at[0, OWN, i, 6], kv.at[0, OWN, i, 2]
        return [rcopy(lo, kv.at[0, OWN, i, 5], gb_s.at[i, 0], g_r.at[i, 5], at(0, 1)),
                rcopy(hi, kv.at[0, OWN, i, 3], gb_s.at[i, 1], g_r.at[i, 3], at(0, -1)),
                rcopy((lo, hi)[i], kv.at[0, OWN, i, 4], gb_s.at[i, 2], g_r.at[i, 4], at(0, (2, -2)[i]))]

    def g_c(i, n):
        part = (slice(0, 3), slice(6, 8), slice(3, 6))[n]
        return rcopy(kv.at[0, OWN, i, part], kv.at[0, PREV, i, part], gc_s.at[i, n], gc_r.at[i, n], nx)

    def g_wait(i, d):
        ref = kv.at[0, OWN, i, 0, 1] if d == 0 else kv.at[0, OWN, i, d]
        tag = (gb_s if d in (3, 4, 5) else ga_s).at[i, 0]
        rcopy(ref, ref, tag, g_r.at[i, d], xp).wait_recv()

    def gather_send(i):
        for c in g_a(i):
            c.start()

    def gather_relay(i):
        g_wait(i, 6)
        g_wait(i, 2)
        for c in g_b(i):
            c.start()

    def gather_near(i):
        for d in (0, 1, 7):
            g_wait(i, d)
        g_c(i, 0).start()
        g_c(i, 1).start()

    def gather_last(i):
        for d in (3, 4, 5):
            g_wait(i, d)
        g_c(i, 2).start()

    def gx(h):
        return rcopy(kv.at[h, OWN, :, 0, 0], kv.at[h, OWN, :, 0, 1], gx_s.at[h], gx_r.at[h], xp)

    def gu(h, s):
        src = (NZ - s) % NZ
        if s < 3:
            return rcopy(kv.at[h, OWN, :, src], kv.at[h, OWN, :, src - 1 if src else NZ - 1], gu_s.at[h, s], gu_r.at[h, s], at(0, 1))
        return rcopy(kv.at[h, OWN, 0, 5], kv.at[h, OWN, 0, 4], gu_s.at[h, s], gu_r.at[h, s], at(0, 1))

    def gd(h, s):
        if s < 3:
            return rcopy(kv.at[h, OWN, :, s], kv.at[h, OWN, :, s + 1], gd_s.at[h, s], gd_r.at[h, s], at(0, -1))
        return rcopy(kv.at[h, OWN, 1, 3], kv.at[h, OWN, 1, 4], gd_s.at[h, s], gd_r.at[h, s], at(0, -1))

    def gn(h, d):
        return rcopy(kv.at[h, OWN, :, d], kv.at[h, PREV, :, d], gn_s.at[h], gn_r.at[h], nx)

    def gn_all(h):
        return rcopy(kv.at[h, OWN], kv.at[h, PREV], gn_s.at[h], gn_r.at[h], nx)

    def ring(h, s):
        if h >= KVH:
            return
        if s == 0:
            gx(h).wait_recv()
            gu(h, 0).start()
            gd(h, 0).start()
            gn(h, 0).start()
            return
        gu(h, s - 1).wait_recv()
        if s < 4:
            gu(h, s).start()
        gd(h, s - 1).wait_recv()
        if s < 4:
            gd(h, s).start()
            gn(h, NZ - s).start()
        gn(h, s).start()

    def pos_x():
        return rcopy(posb.at[OWN, 0], posb.at[OWN, 1], px_s, px_r, xp)

    def pos_b():
        return rcopy(posb.at[OWN], posb.at[PREV], pb_s, pb_r, nx)

    gather_send(0)
    pos_x().start()
    for h in range(1, KVH):
        gx(h).start()

    lane = lax.broadcasted_iota(jnp.int32, (T, 128), 1)
    row = lax.broadcasted_iota(jnp.int32, (T, 128), 0)
    eye = jnp.where(lane == row, 1.0, 0.0).astype(B16)
    ones = jnp.where(lax.broadcasted_iota(jnp.int32, (256, 128), 1) < 3, 1.0, 0.0).astype(B16)
    for g in range(G):
        for h in range(KVH):
            qa[h, g * T:(g + 1) * T, HD:] = eye

    for c in loads:
        c.wait()

    def prep_rows(h):
        for g in range(G):
            sl = pl.ds(h * (G * HD) + g * HD if isinstance(h, int) else pl.multiple_of(h * (G * HD) + g * HD, HD), HD)
            rs = pl.ds(g * T, T)
            qa[h, rs, :HD] = q_v[:, sl]
            gg = g_v[:, sl]
            ga[h, rs, :HD] = gg
            d = -jnp.sum(gg.astype(F32) * o_v[:, sl].astype(F32), axis=1, keepdims=True)
            d1 = d.astype(B16)
            e = d - d1.astype(F32)
            d2 = e.astype(B16)
            d3 = e - d2.astype(F32)
            ga[h, rs, HD:] = jnp.where(lane == 0, d1.astype(F32), jnp.where(lane == 1, d2.astype(F32), jnp.where(lane == 2, d3, 0.0))).astype(B16)

    def make_mask(s):
        for d in range(NZ):
            first = T * lax.rem(z + d, NZ)
            for x in range(2):
                kp = posb[s, x, 0:1, :] + first + row
                qp = posb[OWN, 0, 0:1, :] + T * z + lane
                mk[pl.ds(s * HALF + d * 128 + x * T, T), :] = jnp.where(kp <= qp, 0.0, HIDE).astype(B16)

    def r_p(h, d):
        return rcopy(sp_p.at[h, d], rp_p.at[h, d], rp_s.at[h, d], rp_r.at[h, d], pb)

    def r_a(h):
        return [rcopy(s_a2.at[h, 0], r_a2.at[h, 0], ra_s.at[h, 2], ra_r.at[h, 2], at(0, 2)),
                rcopy(s_a2.at[h, 1], r_a2.at[h, 1], ra_s.at[h, 3], ra_r.at[h, 3], at(0, -2)),
                rcopy(s_a1.at[h, 0], r_a1.at[h, 0], ra_s.at[h, 0], ra_r.at[h, 0], at(0, 1)),
                rcopy(s_a1.at[h, 1], r_a1.at[h, 1], ra_s.at[h, 1], ra_r.at[h, 1], at(0, -1))]

    def r_b_copy(h, i, x):
        step = (2, -2, 1, -1, 0)[i]
        return rcopy(s_b.at[h, i, x], r_b.at[h, i, x], rb_s.at[h, i, x], rb_r.at[h, i], at(x, step))

    def term(h, d, i):
        return acc[h, d, i] + rp_p[h, d, i].astype(F32)

    def reduce_first(h):
        for d in (4, 3, 5):
            r_p(h, d).wait_recv()
        for i in range(2):
            s_a2[h, i] = term(h, 4, i).astype(B16)
            s_a1[h, 0, i] = term(h, 3, i).astype(B16)
            s_a1[h, 1, i] = term(h, 5, i).astype(B16)
        for c in r_a(h):
            c.start()

    def reduce_relay(h):
        for d in (1, 7, 0):
            r_p(h, d).wait_recv()
        for j, d in ((2, 1), (3, 7), (4, 0)):
            for i in range(2):
                t = term(h, d, i)
                if j == 4:
                    acc[h, 0, i] = t
                    s_b[h, j, 1, i] = t[T:].astype(B16)
                else:
                    s_b[h, j, 0, i] = t[:T].astype(B16)
                    s_b[h, j, 1, i] = t[T:].astype(B16)
        for j in (2, 3, 4):
            for x in range(2):
                if j < 4 or x == 1:
                    r_b_copy(h, j, x).start()
        for d in (2, 6):
            r_p(h, d).wait_recv()
        for c in r_a(h):
            c.wait_recv()
        for j, d in ((0, 2), (1, 6)):
            for i in range(2):
                t = term(h, d, i) + r_a1[h, j, i].astype(F32)
                if i == j:
                    t = t + r_a2[h, j].astype(F32)
                s_b[h, j, 0, i] = t[:T].astype(B16)
                s_b[h, j, 1, i] = t[T:].astype(B16)
            for x in range(2):
                r_b_copy(h, j, x).start()

    def reduce_last(h):
        for j in (2, 3, 4, 0, 1):
            if j == 4:
                r_b_copy(h, 4, 1).wait_recv()
            else:
                rcopy(s_b.at[h, j], r_b.at[h, j], rb_s.at[h, j, 0], rb_r.at[h, j], xp).wait_recv()
        cs = pl.ds(h * HD if isinstance(h, int) else pl.multiple_of(h * HD, HD), HD)
        for i in range(2):
            t = acc[h, 0, i, 0:T, :]
            for j in range(5):
                for x in range(2):
                    if j < 4 or x == 1:
                        t = t + r_b[h, j, x, i].astype(F32)
            if i == 0:
                dk_ref[:, cs] = (t * SCALE).astype(B16)
            else:
                dv_ref[:, cs] = t.astype(B16)

    cc = SCALE * LOG2E

    def score_tile(h, j):
        s_, e = j // 4, j % 4
        js = pl.ds(j * 256, 256)
        kk = jnp.concatenate([kv[h, s_, 0, 2 * e:2 * e + 2].reshape(256, HD), mk[js, :]], axis=1)
        for r in range(R // C1):
            rs = pl.ds(r * C1, C1)
            s = dot(kk, qa[h, rs, :], NT)
            m = jnp.max(jnp.max(s.reshape(32, 8, C1), axis=0), axis=0, keepdims=True)
            p = jnp.exp2((s - m) * cc)
            p_sc[js, rs] = p
            m_sc[j:j + 1, rs] = m
            l_sc[j:j + 1, rs] = jnp.sum(jnp.sum(p.reshape(32, 8, C1), axis=0), axis=0, keepdims=True)

    def score_end():
        m = m_sc[...]
        c = jnp.exp2((m - jnp.max(m, axis=0, keepdims=True)) * cc)
        sc[...] = c * (1.0 / jnp.sum(c * l_sc[...], axis=0, keepdims=True))

    def key_tile(h, t):
        d = ORDER[t]
        w = jnp.concatenate([p_sc[pl.ds(s_ * HALF + d * 128, 128), :] * sc[s_ * 4 + d // 2:s_ * 4 + d // 2 + 1, :] for s_ in range(2)], axis=0)
        vt = jnp.concatenate([jnp.concatenate([kv[h, s_, 1, d].reshape(128, HD) for s_ in range(2)], axis=0), ones], axis=1)
        dp = dot(vt, ga[h], NT)
        ds_ = (w * dp).astype(B16)
        pv = dot(w.astype(B16), ga[h, :, :HD])
        pk = dot(ds_, qa[h, :, :HD])
        ds_sc[h, d] = ds_
        for i, a in enumerate((pk, pv)):
            sp_p[h, d, i] = a[:128].astype(B16)
            acc[h, d, i] = a[128:]
        r_p(h, d).start()

    def finish_queries(h):
        kt = jnp.concatenate([kv[h, s_, 0, d].reshape(128, HD) for d in range(NZ) for s_ in range(2)], axis=0).T
        for r in range(R // 256):
            dq = (dot(kt, ds_sc[h, :, :, r * 256:(r + 1) * 256].reshape(NK, 256)) * SCALE).T.astype(B16)
            for e in range(4):
                c0 = (h * G + r * 4 + e) * HD
                dq_v[:, c0:c0 + HD] = dq[e * T:(e + 1) * T]

    def head(h):
        if h:
            gn_all(h).wait_recv()
            for j in range(0, 3):
                score_tile(h, j)
            if h > 1:
                reduce_last(h - 2)
            if h == 1:
                ring(2, 4)
                ring(3, 3)
            for j in range(3, 8):
                score_tile(h, j)
            score_end()
        key_tile(h, 0)
        if h == 0:
            ring(1, 3)
            ring(2, 2)
            ring(3, 1)
        key_tile(h, 1)
        key_tile(h, 2)
        if h:
            reduce_relay(h - 1)
        key_tile(h, 3)
        key_tile(h, 4)
        key_tile(h, 5)
        key_tile(h, 6)
        if h == 0:
            ring(1, 4)
            ring(2, 3)
            ring(3, 2)
        if h == 1:
            ring(3, 4)
        if h < KVH - 1:
            reduce_first(h)
        key_tile(h, 7)
        if h == KVH - 1:
            reduce_first(h)

    for h in range(KVH):
        prep_rows(h)
    pos_x().wait_recv()
    pos_b().start()
    make_mask(OWN)
    gather_relay(0)
    gather_send(1)
    gather_near(0)
    ring(1, 0)
    score_tile(0, 4)
    score_tile(0, 7)
    gather_last(0)
    gather_relay(1)
    gather_near(1)
    ring(2, 0)
    score_tile(0, 5)
    score_tile(0, 6)
    pos_b().wait_recv()
    make_mask(PREV)
    ring(1, 1)
    g_c(0, 0).wait_recv()
    g_c(0, 1).wait_recv()
    score_tile(0, 0)
    score_tile(0, 3)
    g_c(0, 2).wait_recv()
    score_tile(0, 1)
    score_tile(0, 2)
    score_end()
    gather_last(1)
    ring(1, 2)
    ring(2, 1)
    ring(3, 0)
    for n in range(3):
        g_c(1, n).wait_recv()

    for h in range(KVH):
        head(h)

    for h in range(KVH - 1):
        finish_queries(h)
    reduce_last(KVH - 2)
    reduce_relay(KVH - 1)
    finish_queries(KVH - 1)
    out = pltpu.make_async_copy(dq_v, dq_hbm, out_sem)
    out.start()
    reduce_last(KVH - 1)

    out.wait()
    pos_x().wait_send()
    pos_b().wait_send()
    for h in range(KVH):
        if h == 0:
            sent = [c for i in range(2) for c in g_a(i) + g_b(i) + [g_c(i, n) for n in range(3)]]
        else:
            sent = [gx(h), gn_all(h)] + [gu(h, s) for s in range(4)] + [gd(h, s) for s in range(4)]
        for c in sent + [r_p(h, d) for d in range(NZ)] + r_a(h):
            c.wait_send()
        for j in range(5):
            for x in range(2):
                if j < 4 or x == 1:
                    r_b_copy(h, j, x).wait_send()


def solution(mesh):
    nblk = mesh.shape["blk"]
    vm = pl.BlockSpec(memory_space=pltpu.VMEM)
    hb = pl.BlockSpec(memory_space=pl.ANY)
    dma = pltpu.SemaphoreType.DMA

    def local(q, k, v, o, g, pos):
        dt = q.dtype
        return pl.pallas_call(
            functools.partial(kernel, nblk),
            out_shape=(jax.ShapeDtypeStruct((T, QH * HD), dt), jax.ShapeDtypeStruct((T, KVH * HD), dt), jax.ShapeDtypeStruct((T, KVH * HD), dt)),
            in_specs=[hb, hb, hb, vm, vm, vm],
            out_specs=(hb, vm, vm),
            scratch_shapes=[
                pltpu.VMEM((T, QH * HD), B16), pltpu.VMEM((T, QH * HD), B16), pltpu.VMEM((T, QH * HD), B16), pltpu.VMEM((T, QH * HD), B16),
                pltpu.VMEM((KVH, 2, 2, NZ, 2, T, HD), B16),
                pltpu.VMEM((2, 2, 8, 128), jnp.int32),
                pltpu.VMEM((NK, 128), B16),
                pltpu.VMEM((KVH, R, 256), B16), pltpu.VMEM((KVH, R, 256), B16),
                pltpu.VMEM((KVH, NZ, 256, R), B16),
                pltpu.VMEM((NK, R), F32),
                pltpu.VMEM((8, R), F32), pltpu.VMEM((8, R), F32), pltpu.VMEM((8, R), F32),
                pltpu.VMEM((KVH, NZ, 2, 128, HD), F32),
                pltpu.VMEM((KVH, NZ, 2, 128, HD), B16), pltpu.VMEM((KVH, NZ, 2, 128, HD), B16),
                pltpu.VMEM((KVH, 2, 2, 128, HD), B16), pltpu.VMEM((KVH, 2, 128, HD), B16),
                pltpu.VMEM((KVH, 2, 2, 128, HD), B16), pltpu.VMEM((KVH, 2, 128, HD), B16),
                pltpu.VMEM((KVH, 5, 2, 2, T, HD), B16), pltpu.VMEM((KVH, 5, 2, 2, T, HD), B16),
                dma((3,)), dma,
                dma((KVH,)), dma((KVH,)), dma((KVH, 4)), dma((KVH, 4)), dma((KVH, 4)), dma((KVH, 4)), dma((KVH,)), dma((KVH,)),
                dma((2, 9)), dma((2, 3)), dma((2, 3)), dma((2, NZ)), dma((2, 3)),
                dma, dma, dma, dma,
                dma((KVH, NZ)), dma((KVH, NZ)),
                dma((KVH, 4)), dma((KVH, 4)), dma((KVH, 5, 2)), dma((KVH, 5)),
            ],
            compiler_params=pltpu.CompilerParams(collective_id=0, has_side_effects=True, vmem_limit_bytes=60 * 2 ** 20),
            cost_estimate=pl.CostEstimate(flops=12 * 10 ** 9, bytes_accessed=6 * 10 ** 6, transcendentals=9 * 10 ** 6),
        )(q, g, o, k, v, pos.reshape(1, T))

    spec = P(("blk", "uly"), None)
    return jax.shard_map(local, mesh=mesh, in_specs=(spec,) * 5 + (P(("blk", "uly")),), out_specs=(spec,) * 3, check_vma=False)
```

```python
import functools

import jax
import jax.numpy as jnp
from jax import lax
from jax.experimental import pallas as pl
from jax.experimental.pallas import tpu as pltpu
from jax.sharding import PartitionSpec as P

MESH = pl.DeviceIdType.MESH
B16 = jnp.bfloat16
F32 = jnp.float32
QH, KVH, HD = 64, 4, 128
G = QH // KVH
T = 64
NZ = 8
R = G * T
NK = 2048
HALF = NK // 2
PREV, OWN = 0, 1
SCALE = HD ** -0.5
LOG2E = 1.4426950408889634
HIDE = -1e30
C1 = 256
NT = (((1,), (1,)), ((), ()))
NN = (((1,), (0,)), ((), ()))
ORDER = (4, 3, 5, 2, 6, 1, 7, 0)


def dot(a, b, dims=NN):
    return lax.dot_general(a, b, dims, preferred_element_type=F32)


def kernel(nblk, q_hbm, g_hbm, o_hbm, k_ref, v_ref, pos_ref, dq_hbm, dk_ref, dv_ref,
           q_v, g_v, o_v, dq_v, kv, posb, mk, qa, ga, ds_sc, p_sc, sc, m_sc, l_sc,
           acc, sp_p, rp_p, s_a1, s_a2, r_a1, r_a2, s_b, r_b,
           in_sem, out_sem, gx_s, gx_r, gu_s, gu_r, gd_s, gd_r, gn_s, gn_r, ga_s, gb_s, gc_s, g_r, gc_r, px_s, px_r, pb_s, pb_r,
           rp_s, rp_r, ra_s, ra_r, rb_s, rb_r):
    b = lax.axis_index("blk")
    u = lax.axis_index("uly")
    z = lax.rem(u, NZ)
    xh = u // NZ
    def at(other, step):
        return (b, (1 - xh if other else xh) * NZ + lax.rem(z + step + NZ, NZ))

    near = [at(x, i) for x in (0, 1) for i in (0, 1, -1, 2, -2)][1:]
    xp = at(1, 0)
    nx = (lax.rem(b + 1, nblk), u)
    pb = (lax.rem(b + nblk - 1, nblk), u)

    def rcopy(src, dst, ss, rs, dev):
        return pltpu.make_async_remote_copy(src_ref=src, dst_ref=dst, send_sem=ss, recv_sem=rs,
                                            device_id=dev, device_id_type=MESH)

    loads = [pltpu.make_async_copy(a, c, in_sem.at[i])
             for i, (a, c) in enumerate(((q_hbm, q_v), (g_hbm, g_v), (o_hbm, o_v)))]
    for c in loads:
        c.start()
    for h in range(KVH):
        kv[h, OWN, 0, 0, 0] = k_ref[:, h * HD:(h + 1) * HD]
        kv[h, OWN, 1, 0, 0] = v_ref[:, h * HD:(h + 1) * HD]
    base = jnp.min(pos_ref[...], axis=1, keepdims=True) - T * z
    posb[OWN, 0] = jnp.broadcast_to(base, (8, 128))

    barrier = pltpu.get_barrier_semaphore()
    for dev in near + [nx, pb]:
        pl.semaphore_signal(barrier, inc=1, device_id=dev, device_id_type=MESH)
    pl.semaphore_wait(barrier, 11)

    def g_a(i):
        own = kv.at[0, OWN, i, 0, 0]
        out = [rcopy(own, kv.at[0, OWN, i, 0, 1], ga_s.at[i, 0], g_r.at[i, 0], xp)]
        for n, step in enumerate((2, -2, 1, -1)):
            for x in range(2):
                d = (NZ - step) % NZ
                out.append(rcopy(own, kv.at[0, OWN, i, d, x], ga_s.at[i, 1 + 2 * n + x], g_r.at[i, d], at(x, step)))
        return out

    def g_b(i):
        lo, hi = kv.at[0, OWN, i, 6], kv.at[0, OWN, i, 2]
        return [rcopy(lo, kv.at[0, OWN, i, 5], gb_s.at[i, 0], g_r.at[i, 5], at(0, 1)),
                rcopy(hi, kv.at[0, OWN, i, 3], gb_s.at[i, 1], g_r.at[i, 3], at(0, -1)),
                rcopy((lo, hi)[i], kv.at[0, OWN, i, 4], gb_s.at[i, 2], g_r.at[i, 4], at(0, (2, -2)[i]))]

    def g_c(i, n):
        part = (slice(0, 3), slice(6, 8), slice(3, 6))[n]
        return rcopy(kv.at[0, OWN, i, part], kv.at[0, PREV, i, part], gc_s.at[i, n], gc_r.at[i, n], nx)

    def g_wait(i, d):
        ref = kv.at[0, OWN, i, 0, 1] if d == 0 else kv.at[0, OWN, i, d]
        tag = (gb_s if d in (3, 4, 5) else ga_s).at[i, 0]
        rcopy(ref, ref, tag, g_r.at[i, d], xp).wait_recv()

    def gather_send(i):
        for c in g_a(i):
            c.start()

    def gather_relay(i):
        g_wait(i, 6)
        g_wait(i, 2)
        for c in g_b(i):
            c.start()

    def gather_near(i):
        for d in (0, 1, 7):
            g_wait(i, d)
        g_c(i, 0).start()
        g_c(i, 1).start()

    def gather_last(i):
        for d in (3, 4, 5):
            g_wait(i, d)
        g_c(i, 2).start()

    def gx(h):
        return rcopy(kv.at[h, OWN, :, 0, 0], kv.at[h, OWN, :, 0, 1], gx_s.at[h], gx_r.at[h], xp)

    def gu(h, s):
        src = (NZ - s) % NZ
        if s < 3:
            return rcopy(kv.at[h, OWN, :, src], kv.at[h, OWN, :, src - 1 if src else NZ - 1], gu_s.at[h, s], gu_r.at[h, s], at(0, 1))
        return rcopy(kv.at[h, OWN, 0, 5], kv.at[h, OWN, 0, 4], gu_s.at[h, s], gu_r.at[h, s], at(0, 1))

    def gd(h, s):
        if s < 3:
            return rcopy(kv.at[h, OWN, :, s], kv.at[h, OWN, :, s + 1], gd_s.at[h, s], gd_r.at[h, s], at(0, -1))
        return rcopy(kv.at[h, OWN, 1, 3], kv.at[h, OWN, 1, 4], gd_s.at[h, s], gd_r.at[h, s], at(0, -1))

    def gn(h, d):
        return rcopy(kv.at[h, OWN, :, d], kv.at[h, PREV, :, d], gn_s.at[h], gn_r.at[h], nx)

    def gn_all(h):
        return rcopy(kv.at[h, OWN], kv.at[h, PREV], gn_s.at[h], gn_r.at[h], nx)

    def ring(h, s):
        if h >= KVH:
            return
        if s == 0:
            gx(h).wait_recv()
            gu(h, 0).start()
            gd(h, 0).start()
            gn(h, 0).start()
            return
        gu(h, s - 1).wait_recv()
        if s < 4:
            gu(h, s).start()
        gd(h, s - 1).wait_recv()
        if s < 4:
            gd(h, s).start()
            gn(h, NZ - s).start()
        gn(h, s).start()

    def pos_x():
        return rcopy(posb.at[OWN, 0], posb.at[OWN, 1], px_s, px_r, xp)

    def pos_b():
        return rcopy(posb.at[OWN], posb.at[PREV], pb_s, pb_r, nx)

    gather_send(0)
    pos_x().start()
    for h in range(1, KVH):
        gx(h).start()

    lane = lax.broadcasted_iota(jnp.int32, (T, 128), 1)
    row = lax.broadcasted_iota(jnp.int32, (T, 128), 0)
    eye = jnp.where(lane == row, 1.0, 0.0).astype(B16)
    ones = jnp.where(lax.broadcasted_iota(jnp.int32, (256, 128), 1) < 3, 1.0, 0.0).astype(B16)
    for g in range(G):
        for h in range(KVH):
            qa[h, g * T:(g + 1) * T, HD:] = eye

    for c in loads:
        c.wait()

    def prep_rows(h):
        for g in range(G):
            sl = pl.ds(h * (G * HD) + g * HD if isinstance(h, int) else pl.multiple_of(h * (G * HD) + g * HD, HD), HD)
            rs = pl.ds(g * T, T)
            qa[h, rs, :HD] = q_v[:, sl]
            gg = g_v[:, sl]
            ga[h, rs, :HD] = gg
            d = -jnp.sum(gg.astype(F32) * o_v[:, sl].astype(F32), axis=1, keepdims=True)
            d1 = d.astype(B16)
            e = d - d1.astype(F32)
            d2 = e.astype(B16)
            d3 = e - d2.astype(F32)
            ga[h, rs, HD:] = jnp.where(lane == 0, d1.astype(F32), jnp.where(lane == 1, d2.astype(F32), jnp.where(lane == 2, d3, 0.0))).astype(B16)

    def make_mask(s):
        for d in range(NZ):
            first = T * lax.rem(z + d, NZ)
            for x in range(2):
                kp = posb[s, x, 0:1, :] + first + row
                qp = posb[OWN, 0, 0:1, :] + T * z + lane
                mk[pl.ds(s * HALF + d * 128 + x * T, T), :] = jnp.where(kp <= qp, 0.0, HIDE).astype(B16)

    def r_p(h, d):
        return rcopy(sp_p.at[h, d], rp_p.at[h, d], rp_s.at[h, d], rp_r.at[h, d], pb)

    def r_a(h):
        return [rcopy(s_a2.at[h, 0], r_a2.at[h, 0], ra_s.at[h, 2], ra_r.at[h, 2], at(0, 2)),
                rcopy(s_a2.at[h, 1], r_a2.at[h, 1], ra_s.at[h, 3], ra_r.at[h, 3], at(0, -2)),
                rcopy(s_a1.at[h, 0], r_a1.at[h, 0], ra_s.at[h, 0], ra_r.at[h, 0], at(0, 1)),
                rcopy(s_a1.at[h, 1], r_a1.at[h, 1], ra_s.at[h, 1], ra_r.at[h, 1], at(0, -1))]

    def r_b_copy(h, i, x):
        step = (2, -2, 1, -1, 0)[i]
        return rcopy(s_b.at[h, i, x], r_b.at[h, i, x], rb_s.at[h, i, x], rb_r.at[h, i], at(x, step))

    def term(h, d, i):
        return acc[h, d, i] + rp_p[h, d, i].astype(F32)

    def reduce_first(h):
        for d in (4, 3, 5):
            r_p(h, d).wait_recv()
        for i in range(2):
            s_a2[h, i] = term(h, 4, i).astype(B16)
            s_a1[h, 0, i] = term(h, 3, i).astype(B16)
            s_a1[h, 1, i] = term(h, 5, i).astype(B16)
        for c in r_a(h):
            c.start()

    def reduce_near(h):
        for d in (1, 7, 0):
            r_p(h, d).wait_recv()
        for j, d in ((2, 1), (3, 7), (4, 0)):
            for i in range(2):
                t = term(h, d, i)
                if j == 4:
                    acc[h, 0, i] = t
                    s_b[h, j, 1, i] = t[T:].astype(B16)
                else:
                    s_b[h, j, 0, i] = t[:T].astype(B16)
                    s_b[h, j, 1, i] = t[T:].astype(B16)
        for j in (2, 3, 4):
            for x in range(2):
                if j < 4 or x == 1:
                    r_b_copy(h, j, x).start()

    def reduce_far(h):
        for d in (2, 6):
            r_p(h, d).wait_recv()
        for c in r_a(h):
            c.wait_recv()
        for j, d in ((0, 2), (1, 6)):
            for i in range(2):
                t = term(h, d, i) + r_a1[h, j, i].astype(F32)
                if i == j:
                    t = t + r_a2[h, j].astype(F32)
                s_b[h, j, 0, i] = t[:T].astype(B16)
                s_b[h, j, 1, i] = t[T:].astype(B16)
            for x in range(2):
                r_b_copy(h, j, x).start()

    def reduce_relay(h):
        reduce_near(h)
        reduce_far(h)

    def reduce_last(h):
        for j in (2, 3, 4, 0, 1):
            if j == 4:
                r_b_copy(h, 4, 1).wait_recv()
            else:
                rcopy(s_b.at[h, j], r_b.at[h, j], rb_s.at[h, j, 0], rb_r.at[h, j], xp).wait_recv()
        cs = pl.ds(h * HD if isinstance(h, int) else pl.multiple_of(h * HD, HD), HD)
        for i in range(2):
            t = acc[h, 0, i, 0:T, :]
            for j in range(5):
                for x in range(2):
                    if j < 4 or x == 1:
                        t = t + r_b[h, j, x, i].astype(F32)
            if i == 0:
                dk_ref[:, cs] = (t * SCALE).astype(B16)
            else:
                dv_ref[:, cs] = t.astype(B16)

    cc = SCALE * LOG2E

    def score_tile(h, j):
        s_, e = j // 4, j % 4
        js = pl.ds(j * 256, 256)
        kk = jnp.concatenate([kv[h, s_, 0, 2 * e:2 * e + 2].reshape(256, HD), mk[js, :]], axis=1)
        for r in range(R // C1):
            rs = pl.ds(r * C1, C1)
            s = dot(kk, qa[h, rs, :], NT)
            m = jnp.max(jnp.max(s.reshape(32, 8, C1), axis=0), axis=0, keepdims=True)
            p = jnp.exp2((s - m) * cc)
            p_sc[js, rs] = p
            m_sc[j:j + 1, rs] = m
            l_sc[j:j + 1, rs] = jnp.sum(jnp.sum(p.reshape(32, 8, C1), axis=0), axis=0, keepdims=True)

    def score_end():
        m = m_sc[...]
        c = jnp.exp2((m - jnp.max(m, axis=0, keepdims=True)) * cc)
        sc[...] = c * (1.0 / jnp.sum(c * l_sc[...], axis=0, keepdims=True))

    def key_tile(h, t):
        d = ORDER[t]
        w = jnp.concatenate([p_sc[pl.ds(s_ * HALF + d * 128, 128), :] * sc[s_ * 4 + d // 2:s_ * 4 + d // 2 + 1, :] for s_ in range(2)], axis=0)
        vt = jnp.concatenate([jnp.concatenate([kv[h, s_, 1, d].reshape(128, HD) for s_ in range(2)], axis=0), ones], axis=1)
        dp = dot(vt, ga[h], NT)
        ds_ = (w * dp).astype(B16)
        pv = dot(w.astype(B16), ga[h, :, :HD])
        pk = dot(ds_, qa[h, :, :HD])
        ds_sc[h, d] = ds_
        for i, a in enumerate((pk, pv)):
            sp_p[h, d, i] = a[:128].astype(B16)
            acc[h, d, i] = a[128:]
        r_p(h, d).start()

    def finish_queries(h):
        kt = jnp.concatenate([kv[h, s_, 0, d].reshape(128, HD) for d in range(NZ) for s_ in range(2)], axis=0).T
        for r in range(R // 256):
            dq = (dot(kt, ds_sc[h, :, :, r * 256:(r + 1) * 256].reshape(NK, 256)) * SCALE).T.astype(B16)
            for e in range(4):
                c0 = (h * G + r * 4 + e) * HD
                dq_v[:, c0:c0 + HD] = dq[e * T:(e + 1) * T]

    def head(h):
        if h:
            gn_all(h).wait_recv()
            for j in range(0, 3):
                score_tile(h, j)
            if h > 1:
                reduce_last(h - 2)
            if h == 1:
                ring(2, 4)
                ring(3, 3)
            for j in range(3, 8):
                score_tile(h, j)
            score_end()
        key_tile(h, 0)
        if h == 0:
            ring(1, 3)
            ring(2, 2)
            ring(3, 1)
        key_tile(h, 1)
        key_tile(h, 2)
        if h:
            reduce_relay(h - 1)
        key_tile(h, 3)
        key_tile(h, 4)
        key_tile(h, 5)
        key_tile(h, 6)
        if h == 0:
            ring(1, 4)
            ring(2, 3)
            ring(3, 2)
        if h == 1:
            ring(3, 4)
        if h < KVH - 1:
            reduce_first(h)
        key_tile(h, 7)
        if h == KVH - 1:
            reduce_first(h)

    for h in range(KVH):
        prep_rows(h)
    pos_x().wait_recv()
    pos_b().start()
    make_mask(OWN)
    gather_relay(0)
    gather_send(1)
    gather_near(0)
    ring(1, 0)
    score_tile(0, 4)
    score_tile(0, 7)
    gather_last(0)
    gather_relay(1)
    gather_near(1)
    ring(2, 0)
    score_tile(0, 5)
    score_tile(0, 6)
    pos_b().wait_recv()
    make_mask(PREV)
    ring(1, 1)
    g_c(0, 0).wait_recv()
    g_c(0, 1).wait_recv()
    score_tile(0, 0)
    score_tile(0, 3)
    g_c(0, 2).wait_recv()
    score_tile(0, 1)
    score_tile(0, 2)
    score_end()
    gather_last(1)
    ring(1, 2)
    ring(2, 1)
    ring(3, 0)
    for n in range(3):
        g_c(1, n).wait_recv()

    for h in range(KVH):
        head(h)

    finish_queries(0)
    finish_queries(1)
    reduce_near(KVH - 1)
    finish_queries(2)
    reduce_far(KVH - 1)
    reduce_last(KVH - 2)
    finish_queries(KVH - 1)
    out = pltpu.make_async_copy(dq_v, dq_hbm, out_sem)
    out.start()
    reduce_last(KVH - 1)

    out.wait()
    pos_x().wait_send()
    pos_b().wait_send()
    for h in range(KVH):
        if h == 0:
            sent = [c for i in range(2) for c in g_a(i) + g_b(i) + [g_c(i, n) for n in range(3)]]
        else:
            sent = [gx(h), gn_all(h)] + [gu(h, s) for s in range(4)] + [gd(h, s) for s in range(4)]
        for c in sent + [r_p(h, d) for d in range(NZ)] + r_a(h):
            c.wait_send()
        for j in range(5):
            for x in range(2):
                if j < 4 or x == 1:
                    r_b_copy(h, j, x).wait_send()


def solution(mesh):
    nblk = mesh.shape["blk"]
    vm = pl.BlockSpec(memory_space=pltpu.VMEM)
    hb = pl.BlockSpec(memory_space=pl.ANY)
    dma = pltpu.SemaphoreType.DMA

    def local(q, k, v, o, g, pos):
        dt = q.dtype
        return pl.pallas_call(
            functools.partial(kernel, nblk),
            out_shape=(jax.ShapeDtypeStruct((T, QH * HD), dt), jax.ShapeDtypeStruct((T, KVH * HD), dt), jax.ShapeDtypeStruct((T, KVH * HD), dt)),
            in_specs=[hb, hb, hb, vm, vm, vm],
            out_specs=(hb, vm, vm),
            scratch_shapes=[
                pltpu.VMEM((T, QH * HD), B16), pltpu.VMEM((T, QH * HD), B16), pltpu.VMEM((T, QH * HD), B16), pltpu.VMEM((T, QH * HD), B16),
                pltpu.VMEM((KVH, 2, 2, NZ, 2, T, HD), B16),
                pltpu.VMEM((2, 2, 8, 128), jnp.int32),
                pltpu.VMEM((NK, 128), B16),
                pltpu.VMEM((KVH, R, 256), B16), pltpu.VMEM((KVH, R, 256), B16),
                pltpu.VMEM((KVH, NZ, 256, R), B16),
                pltpu.VMEM((NK, R), F32),
                pltpu.VMEM((8, R), F32), pltpu.VMEM((8, R), F32), pltpu.VMEM((8, R), F32),
                pltpu.VMEM((KVH, NZ, 2, 128, HD), F32),
                pltpu.VMEM((KVH, NZ, 2, 128, HD), B16), pltpu.VMEM((KVH, NZ, 2, 128, HD), B16),
                pltpu.VMEM((KVH, 2, 2, 128, HD), B16), pltpu.VMEM((KVH, 2, 128, HD), B16),
                pltpu.VMEM((KVH, 2, 2, 128, HD), B16), pltpu.VMEM((KVH, 2, 128, HD), B16),
                pltpu.VMEM((KVH, 5, 2, 2, T, HD), B16), pltpu.VMEM((KVH, 5, 2, 2, T, HD), B16),
                dma((3,)), dma,
                dma((KVH,)), dma((KVH,)), dma((KVH, 4)), dma((KVH, 4)), dma((KVH, 4)), dma((KVH, 4)), dma((KVH,)), dma((KVH,)),
                dma((2, 9)), dma((2, 3)), dma((2, 3)), dma((2, NZ)), dma((2, 3)),
                dma, dma, dma, dma,
                dma((KVH, NZ)), dma((KVH, NZ)),
                dma((KVH, 4)), dma((KVH, 4)), dma((KVH, 5, 2)), dma((KVH, 5)),
            ],
            compiler_params=pltpu.CompilerParams(collective_id=0, has_side_effects=True, vmem_limit_bytes=60 * 2 ** 20),
            cost_estimate=pl.CostEstimate(flops=12 * 10 ** 9, bytes_accessed=6 * 10 ** 6, transcendentals=9 * 10 ** 6),
        )(q, g, o, k, v, pos.reshape(1, T))

    spec = P(("blk", "uly"), None)
    return jax.shard_map(local, mesh=mesh, in_specs=(spec,) * 5 + (P(("blk", "uly")),), out_specs=(spec,) * 3, check_vma=False)
```
